512 devices in a mesh: dp: 16 (over z), tensor: 8 (over x, core), vocab: 4 (over y).
Axes of the slice: x: 4, y: 4, z: 16, core: 2. Of those that a mesh axis runs over, the one named last changes fastest.
Arguments:
- features: bfloat16 [1024, 49152], P('dp', ('tensor', 'vocab')), may hold values from -80 to 80
- fc_weight: bfloat16 [49152, 16384], P(('tensor', 'vocab'), 'dp'), may hold values from -1 to 1
- norm_gain: float32 [16384], P('dp'), may hold values from 0.1 to 1.9
- head_weight: bfloat16 [16384, 16384], P('dp', ('tensor', 'vocab')), may hold values from -4 to 4
- draft_map: int32 [16384], P(('tensor', 'vocab')), may hold values from 0 to 98298, as said below
- drafted: int32 [1024], P('dp'), may hold values from 0 to 114681, as said below
Outputs:
- logprob: float32 [1024, 16384], P('dp', ('tensor', 'vocab'))
- drafted_logp: float32 [1024], P('dp')
The draws below stay inside these ranges and needn't reach their ends.
Inputs may be any that keep to these rules, and one draw needn't show every extreme that they name: Draft id j stands for target id j + draft_map[j]; these target ids start at 0, rise strictly with j and stay below 128256. Every row's drafted id is the target id of exactly one draft id.
All inputs are finite; a program needn't handle non-finite values.
Results may differ from the reference program's by a relative error of at most 0.0029.
Values may be sent and summed in bfloat16 or wider, within the bound.
No kernel may reach another device: no remote copies, remote signals or barrier semaphores. Data moves between devices by JAX's collectives and lax.ppermute only.
A program may use at most 64 MiB of HBM per device.

```python
import jax
import jax.numpy as jnp
from jax import lax

D = 16384
VD = 16384
ROWS = 1024


def target_ids(key):
    gaps = jax.random.randint(key, (VD,), 1, 8)
    target = (jnp.cumsum(gaps) - gaps[0]).astype(jnp.int32)
    return target.at[VD - 1].set(7 * (VD - 1)).astype(jnp.int32)


def draw_features(key, part):
    key = jax.random.fold_in(key, 11)
    first, second = jax.random.split(key)
    base = jnp.clip(jax.random.normal(first, (ROWS, 3 * D), jnp.float32), -6.0, 6.0)
    spread = 10.0 ** (0.5 * jax.random.uniform(second, (ROWS, 1), jnp.float32))
    return (base * spread).astype(jnp.bfloat16)


def draw_fc_weight(key, part):
    key = jax.random.fold_in(key, 23)
    first, second = jax.random.split(key)
    rising = 3.0 ** (jnp.arange(D, dtype=jnp.float32) / (D - 1))
    base = jnp.clip(jax.random.normal(first, (3 * D, D), jnp.float32), -6.0, 6.0)
    spread = 10.0 ** (0.5 * jax.random.uniform(second, (D,), jnp.float32))
    scale = (rising * spread / (3.0 * D) ** 0.5)[None, :]
    return (base * scale / 10.0).astype(jnp.bfloat16)


def draw_head_weight(key, part):
    key = jax.random.fold_in(key, 37)
    base = jnp.clip(jax.random.normal(key, (D, VD), jnp.float32), -6.0, 6.0) * (3.0 / D ** 0.5)
    return base.astype(jnp.bfloat16)


def draw_draft_map(key, part):
    target = target_ids(key)
    return (target - jnp.arange(VD, dtype=jnp.int32)).astype(jnp.int32)


def draw_drafted(key, part):
    target = target_ids(key)
    key = jax.random.fold_in(key, 53)
    chosen = jax.random.randint(key, (ROWS,), 0, VD)
    chosen = chosen.at[0].set(VD - 1).at[1].set(0)
    return target[chosen].astype(jnp.int32)


def setup_inputs(seed: int = 0) -> dict:
    seeds = jax.random.split(jax.random.key(seed), 7)
    features = draw_features(jax.random.fold_in(seeds[6], 71), 0)
    fc_weight = draw_fc_weight(jax.random.fold_in(seeds[6], 71), 0)
    norm_gain = jnp.clip(1.0 + 0.18 * jax.random.normal(seeds[2], (D,), jnp.float32), 0.1, 1.9)
    head_weight = draw_head_weight(jax.random.fold_in(seeds[6], 71), 0)
    draft_map = draw_draft_map(jax.random.fold_in(seeds[6], 71), 0)
    drafted = draw_drafted(jax.random.fold_in(seeds[6], 71), 0)
    return {"features": features, "fc_weight": fc_weight, "norm_gain": norm_gain, "head_weight": head_weight, "draft_map": draft_map, "drafted": drafted}


eps = 1e-05

def reference(features, fc_weight, norm_gain, head_weight, draft_map, drafted):
    joined = jnp.dot(features, fc_weight, preferred_element_type=jnp.float32)
    square = lax.optimization_barrier(jnp.mean(joined * joined, axis=1))
    normed = (joined * lax.rsqrt(square + eps)[:, None] * norm_gain[None, :]).astype(jnp.bfloat16)
    logits = jnp.dot(normed, head_weight, preferred_element_type=jnp.float32)
    top = lax.optimization_barrier(jnp.max(logits, axis=1))
    lse = top + jnp.log(lax.optimization_barrier(jnp.sum(jnp.exp(logits - top[:, None]), axis=1)))
    logprob = logits - lse[:, None]
    target = jnp.arange(VD, dtype=jnp.int32) + draft_map
    hit = drafted[:, None] == target[None, :]
    picked = lax.optimization_barrier(jnp.sum(jnp.where(hit, logits, jnp.float32(0.0)), axis=1))
    return (logprob, picked - lse)
```

```python
import jax
import jax.numpy as jnp
from jax import lax
from jax.sharding import PartitionSpec as P

D = 16384
Z = 16
eps = 1e-05

CHUNKS = 2
ORDERS = (
    (("x", 1), ("x", 3), ("y", 1), ("y", 3)),
    (("y", 1), ("y", 3), ("x", 1), ("x", 3)),
    (("x", 3), ("x", 1), ("y", 3), ("y", 1)),
    (("y", 3), ("y", 1), ("x", 3), ("x", 1)),
)


def send_z(a, by):
    return lax.ppermute(a, "dp", [(i, (i + by) % Z) for i in range(Z)])


def send_core(a):
    return lax.ppermute(a, "tensor", [(i, i ^ 1) for i in range(8)])


def send_plane(a, axis, k):
    if axis == "x":
        return lax.ppermute(a, "tensor", [(i, i ^ (2 * k)) for i in range(8)])
    return lax.ppermute(a, "vocab", [(i, i ^ k) for i in range(4)])


def side(pos, k, first):
    if first and k == 1:
        return (pos >> 1) ^ (pos & 1)
    return pos & 1 if k == 1 else pos >> 1


def sides(order, x, y):
    seen = set()
    out = []
    for axis, k in order:
        out.append(side(x if axis == "x" else y, k, axis not in seen))
        seen.add(axis)
    return out


def plane_scatter(a, order, keep):
    for (axis, k), h in zip(order, keep):
        half = a.shape[0] // 2
        got = send_plane(lax.dynamic_slice_in_dim(a, (1 - h) * half, half, 0), axis, k)
        a = lax.dynamic_slice_in_dim(a, h * half, half, 0) + got
    return a


def plane_gather(a, order, keep):
    for (axis, k), h in reversed(tuple(zip(order, keep))):
        got = send_plane(a, axis, k)
        a = jnp.where(h == 0, jnp.concatenate([a, got]), jnp.concatenate([got, a]))
    return a


def gather_z(own):
    rows = own.shape[0]
    got = {0: own}
    ahead = behind = own
    for s in range(1, 8):
        ahead, behind = send_z(ahead, 1), send_z(behind, -1)
        got[-s], got[s] = ahead, behind
    half = rows // 2
    got[8] = jnp.concatenate([send_z(ahead[:half], 1), send_z(behind[half:], -1)])
    return got


def scatter_z(part):
    half = part[8].shape[0] // 2
    low, high = send_z(part[8][:half], 1), send_z(part[8][half:], -1)
    up = jnp.concatenate([part[7][:half] + low, part[7][half:]])
    down = jnp.concatenate([part[-7][:half], part[-7][half:] + high])
    for s in range(6, -1, -1):
        up, down = send_z(up, 1), send_z(down, -1)
        if s:
            up, down = up + part[s], down + part[-s]
    return part[0] + up + down


def scatter_small(part):
    for step in (8, 4, 2, 1):
        got = send_z(part[step : 2 * step], step)
        part = part[:step] + got
    return part[0]


def merge(stats):
    top = jnp.max(stats[:, 0], axis=0)
    total = jnp.sum(stats[:, 1] * jnp.exp(stats[:, 0] - top), axis=0)
    return jnp.stack([top, total, jnp.sum(stats[:, 2], axis=0)])


def merge_all(own):
    own = merge(jnp.stack([own, send_core(own)]))
    for axis in ("x", "y"):
        own = merge(jnp.stack([own] + [send_plane(own, axis, k) for k in (1, 2, 3)]))
    return own


def body(features, fc_weight, norm_gain, head_weight, draft_map, drafted):
    t, y = lax.axis_index("tensor"), lax.axis_index("vocab")
    x, core = t >> 1, t & 1
    half = fc_weight.shape[1] // 2
    mine, other = core * half, (1 - core) * half
    fc_mine = lax.dynamic_slice_in_dim(fc_weight, mine, half, 1)
    fc_other = lax.dynamic_slice_in_dim(fc_weight, other, half, 1)
    gain_mine = lax.dynamic_slice_in_dim(norm_gain, mine, half, 0)
    gain_other = lax.dynamic_slice_in_dim(norm_gain, other, half, 0)
    head_mine = lax.dynamic_slice_in_dim(head_weight, mine, half, 0)
    head_other = lax.dynamic_slice_in_dim(head_weight, other, half, 0)
    f32 = jnp.float32

    groups = ((0, -1, 1, -2, 2, -3, 3, 4), (-4, -5, 5, -6, 6, -7, 7, 8))
    rows = features.shape[0] // CHUNKS
    logits, squares = [], []
    for c in range(CHUNKS):
        shards = gather_z(features[c * rows : (c + 1) * rows])
        part, square = {}, {}
        for g, members in enumerate(groups):
            order = ORDERS[(2 * c + g) % 4]
            keep = sides(order, x, y)
            block = jnp.concatenate([shards[r] for r in members])
            away = send_core(jnp.dot(block, fc_other, preferred_element_type=f32))
            joined = jnp.dot(block, fc_mine, preferred_element_type=f32) + away
            joined = plane_scatter(joined, order, keep)
            a_mine = plane_gather((joined * gain_mine).astype(jnp.bfloat16), order, keep)
            a_other = send_core(a_mine)
            both = jnp.dot(a_mine, head_mine, preferred_element_type=f32)
            both = both + jnp.dot(a_other, head_other, preferred_element_type=f32)
            sq = jnp.sum((a_mine.astype(f32) / gain_mine) ** 2, axis=1)
            sq = sq + jnp.sum((a_other.astype(f32) / gain_other) ** 2, axis=1)
            for i, r in enumerate(members):
                part[r] = both[i * rows : (i + 1) * rows]
                square[r % Z] = sq[i * rows : (i + 1) * rows]
        logits.append(scatter_z(part))
        squares.append(scatter_small(jnp.stack([square[r] for r in range(Z)])))
    logits = jnp.concatenate(logits)
    square = jnp.concatenate(squares) / D
    logits = logits * lax.rsqrt(square + eps)[:, None]

    width = logits.shape[1]
    target = (
        draft_map + jnp.arange(width, dtype=jnp.int32) + lax.axis_index(("tensor", "vocab")) * width
    )
    hit = drafted[:, None] == target[None, :]
    own_pick = jnp.sum(jnp.where(hit, logits, f32(0.0)), axis=1)
    own_top = jnp.max(logits, axis=1)
    own_total = jnp.sum(jnp.exp(logits - own_top[:, None]), axis=1)
    top, total, picked = merge_all(jnp.stack([own_top, own_total, own_pick]))
    lse = top + jnp.log(total)
    return (logits - lse[:, None], picked - lse)


def solution(mesh):
    placed = (
        P("dp", ("tensor", "vocab")),
        P(("tensor", "vocab"), "dp"),
        P("dp"),
        P("dp", ("tensor", "vocab")),
        P(("tensor", "vocab")),
        P("dp"),
    )
    return jax.shard_map(
        body,
        mesh=mesh,
        in_specs=placed,
        out_specs=(P("dp", ("tensor", "vocab")), P("dp")),
        check_vma=False,
    )
```

```python
import jax
import jax.numpy as jnp
from jax import lax
from jax.sharding import PartitionSpec as P

D = 16384
eps = 1e-05
PLANE = ("tensor", "vocab")
CHUNKS = 2


def scatter(a, axes, exchange):
    if not exchange:
        return lax.psum_scatter(a, axes, scatter_dimension=0, tiled=True)
    n = lax.axis_size(axes)
    got = lax.all_to_all(a, axes, 0, 0, tiled=True)
    return jnp.sum(got.reshape((n, got.shape[0] // n) + got.shape[1:]), axis=0)


def body(features, fc_weight, norm_gain, head_weight, draft_map, drafted):
    f32 = jnp.float32
    rows = features.shape[0] // CHUNKS
    shards = [
        lax.all_gather(features[c * rows : (c + 1) * rows], "dp", axis=0, tiled=True)
        for c in range(CHUNKS)
    ]
    logits, squares = [], []
    for c in range(CHUNKS):
        partial = jnp.dot(shards[c], fc_weight, preferred_element_type=f32)
        joined = scatter(partial, PLANE, c == 1)
        scaled = (joined * norm_gain).astype(jnp.bfloat16)
        scaled = lax.all_gather(scaled, PLANE, axis=0, tiled=True)
        squares.append(jnp.sum((scaled.astype(f32) / norm_gain) ** 2, axis=1))
        both = jnp.dot(scaled, head_weight, preferred_element_type=f32)
        logits.append(scatter(both, "dp", c == 1))
    logits = jnp.concatenate(logits)
    squares = [s.reshape(-1, rows) for s in squares]
    square = jnp.sum(lax.all_to_all(jnp.concatenate(squares, axis=1), "dp", 0, 0, tiled=True), axis=0) / D
    logits = logits * lax.rsqrt(square + eps)[:, None]

    width = logits.shape[1]
    target = draft_map + jnp.arange(width, dtype=jnp.int32) + lax.axis_index(PLANE) * width
    hit = drafted[:, None] == target[None, :]
    own_pick = jnp.sum(jnp.where(hit, logits, f32(0.0)), axis=1)
    own_top = jnp.max(logits, axis=1)
    own_total = jnp.sum(jnp.exp(logits - own_top[:, None]), axis=1)
    own = jnp.stack([own_top, own_total, own_pick])
    every = jnp.broadcast_to(own, (lax.axis_size(PLANE),) + own.shape)
    every = lax.all_to_all(every, PLANE, 0, 0, tiled=True)
    top = jnp.max(every[:, 0], axis=0)
    total = jnp.sum(every[:, 1] * jnp.exp(every[:, 0] - top), axis=0)
    picked = jnp.sum(every[:, 2], axis=0)
    lse = top + jnp.log(total)
    return (logits - lse[:, None], picked - lse)


def solution(mesh):
    placed = (
        P("dp", ("tensor", "vocab")),
        P(("tensor", "vocab"), "dp"),
        P("dp"),
        P("dp", ("tensor", "vocab")),
        P(("tensor", "vocab")),
        P("dp"),
    )
    return jax.shard_map(
        body,
        mesh=mesh,
        in_specs=placed,
        out_specs=(P("dp", ("tensor", "vocab")), P("dp")),
        check_vma=False,
    )
```

```python
import jax
import jax.numpy as jnp
from jax import lax
from jax.sharding import PartitionSpec as P

eps = 1e-05
PLANE = ("tensor", "vocab")
f16, bf16, f32 = jnp.float16, jnp.bfloat16, jnp.float32

UP = 2.0**9
PARTIAL = 2.0**-1
SCALED = 2.0**-7
FINE = 2.0**11


def body(features, fc_weight, norm_gain, head_weight, draft_map, drafted):
    sent = (features.astype(f32) * UP).astype(f16)
    every = lax.all_gather(sent, "dp", axis=0, tiled=True).astype(bf16)
    partial = jnp.dot(every, fc_weight, preferred_element_type=f32)
    partial = (partial * (PARTIAL / UP)).astype(f16)
    n = lax.axis_size(PLANE)
    got = lax.all_to_all(partial, PLANE, 0, 0, tiled=True).reshape(n, -1, partial.shape[1])
    joined = jnp.sum(got.astype(f32), axis=0)
    scaled = (joined * (norm_gain * (SCALED / PARTIAL))).astype(f16)
    scaled = lax.all_gather(scaled, PLANE, axis=0, tiled=True)
    both = jnp.dot(scaled.astype(bf16), head_weight, preferred_element_type=f32)

    own = scaled.astype(f32) * (1.0 / (norm_gain * SCALED))
    level = jnp.log2(jnp.mean(own * own, axis=1) + eps)
    high = level.astype(f16)
    low = ((level - high.astype(f32)) * FINE).astype(f16)
    both = both * (jnp.exp2(-0.5 * high.astype(f32)) / SCALED)[:, None]
    z = lax.axis_size("dp")
    both = both.astype(f16).reshape(z, -1, both.shape[1])
    rows, width = both.shape[1:]
    levels = jnp.stack([high.reshape(z, rows), low.reshape(z, rows)], axis=1)
    levels = jnp.pad(levels, ((0, 0), (0, 6), (0, width - rows)))
    got = lax.all_to_all(jnp.concatenate([both, levels], axis=1), "dp", 0, 0)
    high = got[:, rows, :rows].astype(f32)
    low = got[:, rows + 1, :rows].astype(f32)
    square = jnp.mean(jnp.exp2(high + low * (1.0 / FINE)), axis=0)
    back = jnp.exp2(0.5 * high) * lax.rsqrt(square)
    logits = jnp.sum(got[:, :rows].astype(f32) * back[:, :, None], axis=0)

    target = draft_map + jnp.arange(width, dtype=jnp.int32) + lax.axis_index(PLANE) * width
    hit = drafted[:, None] == target[None, :]
    own_pick = jnp.sum(jnp.where(hit, logits, f32(0.0)), axis=1)
    own_top = jnp.max(logits, axis=1)
    own_total = jnp.sum(jnp.exp(logits - own_top[:, None]), axis=1)
    own = jnp.stack([own_top, own_total, own_pick])
    every = lax.all_to_all(jnp.broadcast_to(own, (n,) + own.shape), PLANE, 0, 0)
    top = jnp.max(every[:, 0], axis=0)
    total = jnp.sum(every[:, 1] * jnp.exp(every[:, 0] - top), axis=0)
    picked = jnp.sum(every[:, 2], axis=0)
    lse = top + jnp.log(total)
    return (logits - lse[:, None], picked - lse)


def solution(mesh):
    placed = (
        P("dp", ("tensor", "vocab")),
        P(("tensor", "vocab"), "dp"),
        P("dp"),
        P("dp", ("tensor", "vocab")),
        P(("tensor", "vocab")),
        P("dp"),
    )
    return jax.shard_map(
        body,
        mesh=mesh,
        in_specs=placed,
        out_specs=(P("dp", ("tensor", "vocab")), P("dp")),
        check_vma=False,
    )
```

```python
import jax
import jax.numpy as jnp
from jax import lax
from jax.sharding import PartitionSpec as P

eps = 1e-05
PLANE = ("tensor", "vocab")
CHUNKS = 2
f16, bf16, f32 = jnp.float16, jnp.bfloat16, jnp.float32

UP = 2.0**9
PARTIAL = 2.0**-2
SCALED = 2.0**-7

CORE_PAIRS = [(i, i ^ 1) for i in range(8)]
SAME_CORE = [[(2 * x + c) * 4 + y for x in range(4) for y in range(4)] for c in range(2)]
PEERS = 16


def exchange(a):
    return lax.all_to_all(a, PLANE, 0, 0, axis_index_groups=SAME_CORE)


def after(a, b):
    return a if b is None else lax.optimization_barrier((a, b))[0]


def body(features, fc_weight, norm_gain, head_weight, draft_map, drafted):
    core = lax.axis_index("tensor") % 2
    z = lax.axis_size("dp")
    sent = (features.astype(f32) * UP).astype(f16)
    every = lax.all_gather(sent, "dp")
    depth = fc_weight.shape[1]
    rows = features.shape[0]
    part = rows // CHUNKS

    def joined_part(first):
        block = lax.dynamic_slice_in_dim(every, first, z // 2, 0).astype(bf16)
        return jnp.dot(block, fc_weight, preferred_element_type=f32) * (PARTIAL / UP)

    away = joined_part((1 - core) * (z // 2)).astype(f16)
    away = lax.ppermute(away, "tensor", CORE_PAIRS)
    chip = (joined_part(core * (z // 2)) + away.astype(f32)).astype(f16)

    logits, squares, sent, both = [], [], None, None
    for c in range(CHUNKS):
        mine = chip[:, c * part : (c + 1) * part].reshape(PEERS, -1, depth)
        got = after(exchange(mine), sent)
        joined = jnp.sum(got.astype(f32), axis=0)
        scaled = (joined * (norm_gain * (SCALED / PARTIAL))).astype(f16)
        sent = jnp.broadcast_to(scaled, (PEERS,) + scaled.shape)
        scaled = after(exchange(sent).reshape(-1, depth), both)
        other = lax.ppermute(scaled, "tensor", CORE_PAIRS)
        scaled = jnp.where(
            core == 0, jnp.concatenate([scaled, other]), jnp.concatenate([other, scaled])
        )
        own = scaled.astype(f32) * (1.0 / (norm_gain * SCALED))
        square = jnp.mean(own * own, axis=1) + eps
        both = jnp.dot(scaled.astype(bf16), head_weight, preferred_element_type=f32)
        both = (both * (lax.rsqrt(square) / SCALED)[:, None]).astype(f16)
        squares.append(square.reshape(z, part))
        logits.append(lax.all_to_all(both.reshape(z, part, -1), "dp", 0, 0))

    square = lax.all_to_all(jnp.concatenate(squares, axis=1), "dp", 0, 0)
    back = jnp.sqrt(square / jnp.mean(square, axis=0))
    logits = [
        jnp.sum(got.astype(f32) * back[:, c * part : (c + 1) * part, None], axis=0)
        for c, got in enumerate(logits)
    ]
    logits = jnp.concatenate(logits)

    width = logits.shape[1]
    target = draft_map + jnp.arange(width, dtype=jnp.int32) + lax.axis_index(PLANE) * width
    hit = drafted[:, None] == target[None, :]
    own_pick = jnp.sum(jnp.where(hit, logits, f32(0.0)), axis=1)
    own_top = jnp.max(logits, axis=1)
    own_total = jnp.sum(jnp.exp(logits - own_top[:, None]), axis=1)
    own = jnp.pad(jnp.stack([own_top, own_total, own_pick]), ((0, 5), (0, 128 - rows)))
    every = lax.all_to_all(jnp.broadcast_to(own, (lax.axis_size(PLANE),) + own.shape), PLANE, 0, 0)
    every = every[:, :, :rows]
    top = jnp.max(every[:, 0], axis=0)
    total = jnp.sum(every[:, 1] * jnp.exp(every[:, 0] - top), axis=0)
    picked = jnp.sum(every[:, 2], axis=0)
    lse = top + jnp.log(total)
    return (logits - lse[:, None], picked - lse)


def solution(mesh):
    placed = (
        P("dp", ("tensor", "vocab")),
        P(("tensor", "vocab"), "dp"),
        P("dp"),
        P("dp", ("tensor", "vocab")),
        P(("tensor", "vocab")),
        P("dp"),
    )
    return jax.shard_map(
        body,
        mesh=mesh,
        in_specs=placed,
        out_specs=(P("dp", ("tensor", "vocab")), P("dp")),
        check_vma=False,
    )
```

```python
import jax
import jax.numpy as jnp
from jax import lax
from jax.sharding import PartitionSpec as P

eps = 1e-05
PLANE = ("tensor", "vocab")
f16, bf16, f32 = jnp.float16, jnp.bfloat16, jnp.float32

UP = 2.0**9
PARTIAL = 2.0**-2
SCALED = 2.0**-7
FINE = 2.0**11

Z = 16
PEERS = 16
CORE_PAIRS = [(i, i ^ 1) for i in range(8)]
SAME_CORE = [[(2 * x + c) * 4 + y for x in range(4) for y in range(4)] for c in range(2)]
SAME_PARITY = [[2 * i + p for i in range(Z // 2)] for p in range(2)]


def swap_cores(a):
    return lax.ppermute(a, "tensor", CORE_PAIRS)


def exchange(a):
    return lax.all_to_all(a, PLANE, 0, 0, axis_index_groups=SAME_CORE)


def pick(a, i):
    return lax.dynamic_index_in_dim(a, i, 1, keepdims=False)


def pack(values, square):
    n, rows, width = values.shape
    level = jnp.log2(square)
    high = level.astype(f16)
    low = ((level - high.astype(f32)) * FINE).astype(f16)
    levels = jnp.pad(jnp.stack([high, low], axis=1), ((0, 0), (0, 6), (0, width - rows)))
    values = (values * lax.rsqrt(square)[:, :, None]).astype(f16)
    return jnp.concatenate([values, levels], axis=1)


def unpack(a):
    rows = a.shape[1] - 8
    high, low = a[:, rows, :rows].astype(f32), a[:, rows + 1, :rows].astype(f32)
    square = jnp.exp2(high + low * (1.0 / FINE))
    return a[:, :rows].astype(f32), square


def body(features, fc_weight, norm_gain, head_weight, draft_map, drafted):
    core = lax.axis_index("tensor") % 2
    parity = lax.axis_index("dp") % 2
    depth = fc_weight.shape[1]
    width = head_weight.shape[1]
    rows = features.shape[0]
    half = rows // 2

    sent = (features.astype(f32) * UP).astype(f16)
    every = lax.all_gather(sent, "dp").reshape(Z, 2, half, -1)

    def joined_part(h):
        block = pick(every, h).astype(bf16)
        return jnp.dot(block, fc_weight, preferred_element_type=f32) * (PARTIAL / UP)

    away = swap_cores(joined_part(1 - core).astype(f16))
    chip = (joined_part(core) + away.astype(f32)).astype(f16)
    head_other = swap_cores(lax.optimization_barrier((head_weight, chip))[0])
    joined = jnp.sum(exchange(chip).astype(f32), axis=0)
    scaled = (joined * (norm_gain * (SCALED / PARTIAL))).astype(f16)
    scaled = exchange(jnp.broadcast_to(scaled, (PEERS,) + scaled.shape))
    own = scaled.astype(f32) * (1.0 / (norm_gain * SCALED))
    square = jnp.mean(own * own, axis=2) + eps
    scaled = scaled.reshape(Z // 2, 2, half, depth)
    square = square.reshape(Z // 2, 2, half)

    def partial(h, weight):
        block = pick(scaled, h).astype(bf16)
        return jnp.dot(block, weight, preferred_element_type=f32) * (1.0 / SCALED)

    def through(weight, by):
        values = partial(1 - parity, weight).reshape(1, -1, width)
        packed = pack(values, pick(square, 1 - parity).reshape(1, -1))
        got, far = unpack(lax.ppermute(packed, "dp", [(i, (i + by) % Z) for i in range(Z)]))
        return got.reshape(Z // 2, half, width), far.reshape(Z // 2, half)

    kept = pick(square, parity)
    sums, squares = [], []
    for weight, (got, far) in (
        (head_weight, through(head_weight, 1)),
        (head_other, through(head_other, -1)),
    ):
        sums.append(partial(parity, weight) + got * jnp.sqrt(far)[:, :, None])
        squares.append(kept + far)
    packed = pack(jnp.concatenate(sums, axis=1), jnp.concatenate(squares, axis=1))
    got, square = unpack(lax.all_to_all(packed, "dp", 0, 0, axis_index_groups=SAME_PARITY))
    back = jnp.sqrt(square / (jnp.sum(square, axis=0) / Z))
    logits = jnp.sum(got * back[:, :, None], axis=0)

    mine, other = logits[:half], swap_cores(logits[half:])
    logits = jnp.where(
        core == 0, jnp.concatenate([mine, other]), jnp.concatenate([other, mine])
    )
    target = draft_map + jnp.arange(width, dtype=jnp.int32) + lax.axis_index(PLANE) * width
    hit = drafted[:, None] == target[None, :]
    own_pick = jnp.sum(jnp.where(hit, logits, f32(0.0)), axis=1)
    own_top = jnp.max(logits, axis=1)
    own_total = jnp.sum(jnp.exp(logits - own_top[:, None]), axis=1)
    own = jnp.pad(jnp.stack([own_top, own_total, own_pick]), ((0, 5), (0, 128 - rows)))
    every = lax.all_to_all(jnp.broadcast_to(own, (lax.axis_size(PLANE),) + own.shape), PLANE, 0, 0)
    every = every[:, :, :rows]
    top = jnp.max(every[:, 0], axis=0)
    total = jnp.sum(every[:, 1] * jnp.exp(every[:, 0] - top), axis=0)
    picked = jnp.sum(every[:, 2], axis=0)
    lse = top + jnp.log(total)
    return (logits - lse[:, None], picked - lse)


def solution(mesh):
    placed = (
        P("dp", ("tensor", "vocab")),
        P(("tensor", "vocab"), "dp"),
        P("dp"),
        P("dp", ("tensor", "vocab")),
        P(("tensor", "vocab")),
        P("dp"),
    )
    return jax.shard_map(
        body,
        mesh=mesh,
        in_specs=placed,
        out_specs=(P("dp", ("tensor", "vocab")), P("dp")),
        check_vma=False,
    )
```

```python
import jax
import jax.numpy as jnp
from jax import lax
from jax.sharding import PartitionSpec as P

eps = 1e-05
PLANE = ("tensor", "vocab")
f16, bf16, f32 = jnp.float16, jnp.bfloat16, jnp.float32

UP = 2.0**9
PARTIAL = 2.0**-2
SCALED = 2.0**-7
LEVEL = 2.0**-7
FINE = 2.0**11

Z = 16
PEERS = 16
CORE_PAIRS = [(i, i ^ 1) for i in range(8)]
SAME_CORE = [[(2 * x + c) * 4 + y for x in range(4) for y in range(4)] for c in range(2)]
SAME_PARITY = [[2 * i + p for i in range(Z // 2)] for p in range(2)]


def swap_cores(a):
    return lax.ppermute(a, "tensor", CORE_PAIRS)


def exchange(a):
    return lax.all_to_all(a, PLANE, 0, 0, axis_index_groups=SAME_CORE)


def pick(a, i):
    return lax.dynamic_index_in_dim(a, i, 1, keepdims=False)


def levels(square, width):
    root = jnp.sqrt(square) * LEVEL
    high = root.astype(f16)
    low = ((root - high.astype(f32)) * FINE).astype(f16)
    pair = jnp.stack([high, low], axis=-2)
    pad = [(0, 0)] * (pair.ndim - 2) + [(0, 6), (0, width - pair.shape[-1])]
    return jnp.pad(pair, pad)


def squares(a, rows):
    high, low = a[..., -8, :rows].astype(f32), a[..., -7, :rows].astype(f32)
    return ((high + low * (1.0 / FINE)) * (1.0 / LEVEL)) ** 2


def body(features, fc_weight, norm_gain, head_weight, draft_map, drafted):
    core = lax.axis_index("tensor") % 2
    parity = lax.axis_index("dp") % 2
    depth = fc_weight.shape[1]
    width = head_weight.shape[1]
    rows = features.shape[0]
    half = rows // 2

    sent = (features.astype(f32) * UP).astype(f16).reshape(2, half, -1)
    every = lax.all_gather(sent, "dp", axis=1)

    def joined_part(h):
        block = lax.dynamic_index_in_dim(every, h, 0, keepdims=False).astype(bf16)
        return jnp.dot(block, fc_weight, preferred_element_type=f32) * (PARTIAL / UP)

    away = joined_part(1 - core).astype(f16)
    kept = lax.optimization_barrier((joined_part(core), away))[0]
    chip = (kept + swap_cores(away).astype(f32)).astype(f16)
    head_other = swap_cores(lax.optimization_barrier((head_weight, chip))[0])
    joined = jnp.sum(exchange(chip).astype(f32), axis=0)
    scaled = (joined * (norm_gain * (SCALED / PARTIAL))).astype(f16)
    scaled = exchange(jnp.broadcast_to(scaled, (PEERS,) + scaled.shape))

    own = scaled.astype(f32) * (1.0 / (norm_gain * SCALED))
    square = (jnp.mean(own * own, axis=2) + eps).reshape(-1)
    head = jnp.concatenate([head_weight, head_other], axis=1)
    logits = jnp.dot(scaled.reshape(-1, depth).astype(bf16), head, preferred_element_type=f32)
    logits = (logits * (lax.rsqrt(square) * (1.0 / SCALED))[:, None]).astype(f16)
    logits = logits.reshape(Z // 2, 2, half, 2 * width)
    square = square.reshape(Z // 2, 2, half)

    far, near = pick(logits, 1 - parity), pick(logits, parity)
    far_level = levels(pick(square, 1 - parity).reshape(-1), width)
    near_square = pick(square, parity).reshape(-1)
    count = near_square.shape[0]
    sums, sum_squares = [], []
    for v, by in ((0, 1), (1, -1)):
        part = slice(v * width, (v + 1) * width)
        got = jnp.concatenate([far[:, :, part].reshape(-1, width), far_level])
        got = lax.ppermute(got, "dp", [(i, (i + by) % Z) for i in range(Z)])
        far_square = squares(got, count)
        both = near_square + far_square
        here, there = jnp.sqrt(near_square / both), jnp.sqrt(far_square / both)
        here = near[:, :, part].reshape(-1, width).astype(f32) * here[:, None]
        got = here + got[:count].astype(f32) * there[:, None]
        sums.append(got.astype(f16).reshape(-1, half, width))
        sum_squares.append(both.reshape(-1, half))
    packed = sums + [levels(jnp.concatenate(sum_squares, axis=1), width)]
    packed = jnp.concatenate(packed, axis=1)
    got = lax.all_to_all(packed, "dp", 0, 0, axis_index_groups=SAME_PARITY)
    square = squares(got, rows)
    back = jnp.sqrt(square / (jnp.sum(square, axis=0) / Z))
    logits = jnp.sum(got[:, :rows].astype(f32) * back[:, :, None], axis=0)

    mine, other = logits[:half], swap_cores(logits[half:])
    logits = jnp.where(
        core == 0, jnp.concatenate([mine, other]), jnp.concatenate([other, mine])
    )
    target = draft_map + jnp.arange(width, dtype=jnp.int32) + lax.axis_index(PLANE) * width
    hit = drafted[:, None] == target[None, :]
    own_pick = jnp.sum(jnp.where(hit, logits, f32(0.0)), axis=1)
    own_top = jnp.max(logits, axis=1)
    own_total = jnp.sum(jnp.exp(logits - own_top[:, None]), axis=1)
    own = jnp.pad(jnp.stack([own_top, own_total, own_pick]), ((0, 5), (0, 128 - rows)))
    every = lax.all_to_all(jnp.broadcast_to(own, (lax.axis_size(PLANE),) + own.shape), PLANE, 0, 0)
    every = every[:, :, :rows]
    top = jnp.max(every[:, 0], axis=0)
    total = jnp.sum(every[:, 1] * jnp.exp(every[:, 0] - top), axis=0)
    picked = jnp.sum(every[:, 2], axis=0)
    lse = top + jnp.log(total)
    return (logits - lse[:, None], picked - lse)


def solution(mesh):
    placed = (
        P("dp", ("tensor", "vocab")),
        P(("tensor", "vocab"), "dp"),
        P("dp"),
        P("dp", ("tensor", "vocab")),
        P(("tensor", "vocab")),
        P("dp"),
    )
    return jax.shard_map(
        body,
        mesh=mesh,
        in_specs=placed,
        out_specs=(P("dp", ("tensor", "vocab")), P("dp")),
        check_vma=False,
    )
```

```python
import jax
import jax.numpy as jnp
from jax import lax
from jax.sharding import PartitionSpec as P

eps = 1e-05
PLANE = ("tensor", "vocab")
f16, bf16, f32 = jnp.float16, jnp.bfloat16, jnp.float32

UP = 2.0**9
PARTIAL = 2.0**-2
SCALED = 2.0**-7
LEVEL = 2.0**-7
FINE = 2.0**11

Z = 16
PEERS = 16
CORE_PAIRS = [(i, i ^ 1) for i in range(8)]
SAME_CORE = [[(2 * x + c) * 4 + y for x in range(4) for y in range(4)] for c in range(2)]
SAME_PARITY = [[2 * i + p for i in range(Z // 2)] for p in range(2)]


def swap_cores(a):
    return lax.ppermute(a, "tensor", CORE_PAIRS)


def by_core(core, mine, other):
    return jnp.where(
        core == 0, jnp.concatenate([mine, other]), jnp.concatenate([other, mine])
    )


def exchange(a):
    return lax.all_to_all(a, PLANE, 0, 0, axis_index_groups=SAME_CORE)


def pick(a, i):
    return lax.dynamic_index_in_dim(a, i, 1, keepdims=False)


def levels(square, width):
    root = jnp.sqrt(square) * LEVEL
    high = root.astype(f16)
    low = ((root - high.astype(f32)) * FINE).astype(f16)
    pair = jnp.stack([high, low], axis=-2)
    pad = [(0, 0)] * (pair.ndim - 2) + [(0, 6), (0, width - pair.shape[-1])]
    return jnp.pad(pair, pad)


def squares(a, rows):
    high, low = a[..., -8, :rows].astype(f32), a[..., -7, :rows].astype(f32)
    return ((high + low * (1.0 / FINE)) * (1.0 / LEVEL)) ** 2


def body(features, fc_weight, norm_gain, head_weight, draft_map, drafted):
    core = lax.axis_index("tensor") % 2
    parity = lax.axis_index("dp") % 2
    depth = fc_weight.shape[1]
    width = head_weight.shape[1]
    rows = features.shape[0]
    half = rows // 2

    sent = (features.astype(f32) * UP).astype(f16).reshape(2, half, -1)
    every = lax.all_gather(sent, "dp", axis=1)

    def joined_part(h):
        block = lax.dynamic_index_in_dim(every, h, 0, keepdims=False).astype(bf16)
        return jnp.dot(block, fc_weight, preferred_element_type=f32) * (PARTIAL / UP)

    away = joined_part(1 - core).astype(f16)
    kept = lax.optimization_barrier((joined_part(core), away))[0]
    chip = (kept + swap_cores(away).astype(f32)).astype(f16)
    later = lax.optimization_barrier((head_weight, draft_map, chip))
    head_other, map_other = swap_cores(later[0]), swap_cores(later[1])
    joined = jnp.sum(exchange(chip).astype(f32), axis=0)
    scaled = (joined * (norm_gain * (SCALED / PARTIAL))).astype(f16)
    scaled = exchange(jnp.broadcast_to(scaled, (PEERS,) + scaled.shape))

    gain = lax.optimization_barrier((norm_gain, map_other))[0]
    own = scaled.astype(f32) * (1.0 / (gain * SCALED))
    square = (jnp.mean(own * own, axis=2) + eps).reshape(Z // 2, 2, half)
    scaled = scaled.reshape(Z // 2, 2, half, depth)

    def partial(h, weight):
        block = pick(scaled, h).astype(bf16).reshape(-1, depth)
        return jnp.dot(block, weight, preferred_element_type=f32)

    far_square = pick(square, 1 - parity).reshape(-1)
    near_square = pick(square, parity).reshape(-1)
    far_level = levels(far_square, width)
    count = far_square.shape[0]

    def through(weight, by):
        values = partial(1 - parity, weight) * (lax.rsqrt(far_square) * (1.0 / SCALED))[:, None]
        values = jnp.concatenate([values.astype(f16), far_level])
        return lax.ppermute(values, "dp", [(i, (i + by) % Z) for i in range(Z)])

    arrived = through(head_weight, 1), through(head_other, -1)
    sums, sum_squares = [], []
    for weight, got in zip((head_weight, head_other), arrived):
        got_square = squares(got, count)
        both = near_square + got_square
        here, there = lax.rsqrt(both) * (1.0 / SCALED), jnp.sqrt(got_square / both)
        got = partial(parity, weight) * here[:, None] + got[:count].astype(f32) * there[:, None]
        sums.append(got.astype(f16).reshape(-1, half, width))
        sum_squares.append(both.reshape(-1, half))
    packed = sums + [levels(jnp.concatenate(sum_squares, axis=1), width)]
    packed = jnp.concatenate(packed, axis=1)
    got = lax.all_to_all(packed, "dp", 0, 0, axis_index_groups=SAME_PARITY)
    square = squares(got, rows)
    back = jnp.sqrt(square / (jnp.sum(square, axis=0) / Z))
    logits = jnp.sum(got[:, :rows].astype(f32) * back[:, :, None], axis=0)

    logits = logits.reshape(2, half, width)
    here = 2 * lax.axis_index("tensor") + 2 * jnp.array([0, 1]) * (1 - 2 * core)
    here = (here * 2 + lax.axis_index("vocab")) * width
    target = jnp.stack([draft_map, map_other]) + jnp.arange(width, dtype=jnp.int32) + here[:, None]
    wanted = lax.dynamic_slice_in_dim(drafted, core * half, half)
    hit = wanted[None, :, None] == target[:, None, :]
    own_pick = jnp.sum(jnp.where(hit, logits, f32(0.0)), axis=(0, 2))
    own_top = jnp.max(logits, axis=(0, 2))
    own_total = jnp.sum(jnp.exp(logits - own_top[None, :, None]), axis=(0, 2))
    own = jnp.pad(jnp.stack([own_top, own_total, own_pick]), ((0, 5), (0, 128 - half)))
    every = exchange(jnp.broadcast_to(own, (PEERS,) + own.shape))[:, :, :half]
    top = jnp.max(every[:, 0], axis=0)
    total = jnp.sum(every[:, 1] * jnp.exp(every[:, 0] - top), axis=0)
    picked = jnp.sum(every[:, 2], axis=0)
    lse = top + jnp.log(total)
    logprob = logits - lse[None, :, None]
    picked = picked - lse
    away = jnp.concatenate([logprob[1], jnp.pad(picked[None], ((0, 7), (0, width - half)))])
    got = swap_cores(away)
    return (
        by_core(core, logprob[0], got[:half]),
        by_core(core, picked, got[half, :half]),
    )


def solution(mesh):
    placed = (
        P("dp", ("tensor", "vocab")),
        P(("tensor", "vocab"), "dp"),
        P("dp"),
        P("dp", ("tensor", "vocab")),
        P(("tensor", "vocab")),
        P("dp"),
    )
    return jax.shard_map(
        body,
        mesh=mesh,
        in_specs=placed,
        out_specs=(P("dp", ("tensor", "vocab")), P("dp")),
        check_vma=False,
    )
```

```python
import jax
import jax.numpy as jnp
from jax import lax
from jax.sharding import PartitionSpec as P

eps = 1e-05
PLANE = ("tensor", "vocab")
f16, bf16, f32 = jnp.float16, jnp.bfloat16, jnp.float32

UP = 2.0**9
PARTIAL = 2.0**-2
SCALED = 2.0**-7
LEVEL = 2.0**-7
FINE = 2.0**11

Z = 16
PEERS = 16
CORE_PAIRS = [(i, i ^ 1) for i in range(8)]
SAME_CORE = [[(2 * x + c) * 4 + y for x in range(4) for y in range(4)] for c in range(2)]
SAME_PARITY = [[2 * i + p for i in range(Z // 2)] for p in range(2)]


def swap_cores(a):
    return lax.ppermute(a, "tensor", CORE_PAIRS)


def by_core(core, mine, other):
    return jnp.where(
        core == 0, jnp.concatenate([mine, other]), jnp.concatenate([other, mine])
    )


def exchange(a):
    return lax.all_to_all(a, PLANE, 0, 0, axis_index_groups=SAME_CORE)


def pick(a, i):
    return lax.dynamic_index_in_dim(a, i, 1, keepdims=False)


def levels(square, width):
    root = jnp.sqrt(square) * LEVEL
    high = root.astype(f16)
    low = ((root - high.astype(f32)) * FINE).astype(f16)
    pair = jnp.stack([high, low], axis=-2)
    pad = [(0, 0)] * (pair.ndim - 2) + [(0, 6), (0, width - pair.shape[-1])]
    return jnp.pad(pair, pad)


def squares(a, rows):
    high, low = a[..., -8, :rows].astype(f32), a[..., -7, :rows].astype(f32)
    return ((high + low * (1.0 / FINE)) * (1.0 / LEVEL)) ** 2


def body(features, fc_weight, norm_gain, head_weight, draft_map, drafted):
    core = lax.axis_index("tensor") % 2
    parity = lax.axis_index("dp") % 2
    depth = fc_weight.shape[1]
    width = head_weight.shape[1]
    rows = features.shape[0]
    half = rows // 2

    sent = (features.astype(f32) * UP).astype(f16).reshape(2, half, -1)
    every = lax.all_gather(sent, "dp", axis=1)

    def joined_part(h):
        block = lax.dynamic_index_in_dim(every, h, 0, keepdims=False).astype(bf16)
        return jnp.dot(block, fc_weight, preferred_element_type=f32) * (PARTIAL / UP)

    away = joined_part(1 - core).astype(f16)
    kept = lax.optimization_barrier((joined_part(core), away))[0]
    chip = (kept + swap_cores(away).astype(f32)).astype(f16)
    later = lax.optimization_barrier((head_weight, draft_map, chip))
    head_other, map_other = swap_cores(later[0]), swap_cores(later[1])
    joined = jnp.sum(exchange(chip).astype(f32), axis=0)
    scaled = (joined * (norm_gain * (SCALED / PARTIAL))).astype(f16)
    scaled = exchange(jnp.broadcast_to(scaled, (PEERS,) + scaled.shape))

    gain = lax.optimization_barrier((norm_gain, map_other))[0]
    own = scaled.astype(f32) * (1.0 / (gain * SCALED))
    square = (jnp.mean(own * own, axis=2) + eps).reshape(Z // 2, 2, half)
    scaled = scaled.reshape(Z // 2, 2, half, depth)

    def partial(h, weight):
        block = pick(scaled, h).astype(bf16).reshape(-1, depth)
        return jnp.dot(block, weight, preferred_element_type=f32)

    far_square = pick(square, 1 - parity).reshape(-1)
    near_square = pick(square, parity).reshape(-1)
    far_level = levels(far_square, width)
    count = far_square.shape[0]

    def through(weight, by):
        values = partial(1 - parity, weight) * (lax.rsqrt(far_square) * (1.0 / SCALED))[:, None]
        values = jnp.concatenate([values.astype(f16), far_level])
        return lax.ppermute(values, "dp", [(i, (i + by) % Z) for i in range(Z)])

    arrived = through(head_weight, 1), through(head_other, -1)
    near = [partial(parity, weight) for weight in (head_weight, head_other)]
    sums, sum_squares = [], []
    for own, got in zip(lax.optimization_barrier(near), arrived):
        got_square = squares(got, count)
        both = near_square + got_square
        here, there = lax.rsqrt(both) * (1.0 / SCALED), jnp.sqrt(got_square / both)
        got = own * here[:, None] + got[:count].astype(f32) * there[:, None]
        sums.append(got.astype(f16).reshape(-1, half, width))
        sum_squares.append(both.reshape(-1, half))
    packed = sums + [levels(jnp.concatenate(sum_squares, axis=1), width)]
    packed = jnp.concatenate(packed, axis=1)
    got = lax.all_to_all(packed, "dp", 0, 0, axis_index_groups=SAME_PARITY)
    square = squares(got, rows)
    back = jnp.sqrt(square / (jnp.sum(square, axis=0) / Z))
    logits = jnp.sum(got[:, :rows].astype(f32) * back[:, :, None], axis=0)

    logits = logits.reshape(2, half, width)
    here = 2 * lax.axis_index("tensor") + 2 * jnp.array([0, 1]) * (1 - 2 * core)
    here = (here * 2 + lax.axis_index("vocab")) * width
    target = jnp.stack([draft_map, map_other]) + jnp.arange(width, dtype=jnp.int32) + here[:, None]
    wanted = lax.dynamic_slice_in_dim(drafted, core * half, half)
    hit = wanted[None, :, None] == target[:, None, :]
    own_pick = jnp.sum(jnp.where(hit, logits, f32(0.0)), axis=(0, 2))
    own_top = jnp.max(logits, axis=(0, 2))
    own_total = jnp.sum(jnp.exp(logits - own_top[None, :, None]), axis=(0, 2))
    own = jnp.pad(jnp.stack([own_top, own_total, own_pick]), ((0, 5), (0, 128 - half)))
    logits = by_core(core, logits[0], swap_cores(logits[1]))
    every = lax.all_to_all(jnp.broadcast_to(own, (2 * PEERS,) + own.shape), PLANE, 0, 0)
    every = every[:, :3, :half].reshape(4, 2, 4, 3, half)
    top = jnp.max(every[:, :, :, 0], axis=(0, 2))
    total = every[:, :, :, 1] * jnp.exp(every[:, :, :, 0] - top[None, :, None])
    lse = (top + jnp.log(jnp.sum(total, axis=(0, 2)))).reshape(rows)
    picked = jnp.sum(every[:, :, :, 2], axis=(0, 2)).reshape(rows)
    return (logits - lse[:, None], picked - lse)


def solution(mesh):
    placed = (
        P("dp", ("tensor", "vocab")),
        P(("tensor", "vocab"), "dp"),
        P("dp"),
        P("dp", ("tensor", "vocab")),
        P(("tensor", "vocab")),
        P("dp"),
    )
    return jax.shard_map(
        body,
        mesh=mesh,
        in_specs=placed,
        out_specs=(P("dp", ("tensor", "vocab")), P("dp")),
        check_vma=False,
    )
```

```python
import jax
import jax.numpy as jnp
from jax import lax
from jax.sharding import PartitionSpec as P

eps = 1e-05
PLANE = ("tensor", "vocab")
f16, bf16, f32 = jnp.float16, jnp.bfloat16, jnp.float32

UP = 2.0**9
PARTIAL = 2.0**-2
LEVEL = 2.0**-7
FINE = 2.0**11

Z = 16
PEERS = 16
CORE_PAIRS = [(i, i ^ 1) for i in range(8)]
SAME_CORE = [[(2 * x + c) * 4 + y for x in range(4) for y in range(4)] for c in range(2)]
SAME_PARITY = [[2 * i + p for i in range(Z // 2)] for p in range(2)]


def swap_cores(a):
    return lax.ppermute(a, "tensor", CORE_PAIRS)


def by_core(core, mine, other):
    return jnp.where(
        core == 0, jnp.concatenate([mine, other]), jnp.concatenate([other, mine])
    )


def exchange(a):
    return lax.all_to_all(a, PLANE, 0, 0, axis_index_groups=SAME_CORE)


def pick(a, i):
    return lax.dynamic_index_in_dim(a, i, 1, keepdims=False)


def levels(square, width):
    root = jnp.sqrt(square) * LEVEL
    high = root.astype(f16)
    low = ((root - high.astype(f32)) * FINE).astype(f16)
    pair = jnp.stack([high, low], axis=-2)
    pad = [(0, 0)] * (pair.ndim - 2) + [(0, 6), (0, width - pair.shape[-1])]
    return jnp.pad(pair, pad)


def squares(a, rows):
    high, low = a[..., -8, :rows].astype(f32), a[..., -7, :rows].astype(f32)
    return ((high + low * (1.0 / FINE)) * (1.0 / LEVEL)) ** 2


def body(features, fc_weight, norm_gain, head_weight, draft_map, drafted):
    core = lax.axis_index("tensor") % 2
    parity = lax.axis_index("dp") % 2
    depth = fc_weight.shape[1]
    width = head_weight.shape[1]
    rows = features.shape[0]
    half = rows // 2

    sent = (features.astype(f32) * UP).astype(f16).reshape(2, half, -1)
    every = lax.all_gather(sent, "dp", axis=1)

    def joined_part(h):
        block = lax.dynamic_index_in_dim(every, h, 0, keepdims=False).astype(bf16)
        return jnp.dot(block, fc_weight, preferred_element_type=f32) * (PARTIAL / UP)

    away = joined_part(1 - core).astype(f16)
    kept = lax.optimization_barrier((joined_part(core), away))[0]
    chip = (kept + swap_cores(away).astype(f32)).astype(f16)
    later = lax.optimization_barrier((head_weight, draft_map, chip))
    head_other, map_other = swap_cores(later[0]), swap_cores(later[1])
    joined = jnp.sum(exchange(chip).astype(f32), axis=0)
    scaled = (joined * (norm_gain * (1.0 / PARTIAL))).astype(bf16)
    scaled = exchange(jnp.broadcast_to(scaled, (PEERS,) + scaled.shape))

    gain = lax.optimization_barrier((norm_gain, map_other))[0]
    own = scaled.astype(f32) * (1.0 / gain)
    square = (jnp.mean(own * own, axis=2) + eps).reshape(Z // 2, 2, half)
    scaled = scaled.reshape(Z // 2, 2, half, depth)

    def partial(h, weight):
        block = pick(scaled, h).reshape(-1, depth)
        return jnp.dot(block, weight, preferred_element_type=f32).reshape(-1, half, width)

    far_square, near_square = pick(square, 1 - parity), pick(square, parity)
    far_level = levels(far_square, width)

    def through(weight, by):
        values = partial(1 - parity, weight) * lax.rsqrt(far_square)[:, :, None]
        values = jnp.concatenate([values.astype(f16), far_level], axis=1)
        return lax.ppermute(values, "dp", [(i, (i + by) % Z) for i in range(Z)])

    arrived = through(head_weight, 1), through(head_other, -1)
    near = [partial(parity, weight) for weight in (head_weight, head_other)]
    sums, sum_squares = [], []
    for own, got in zip(lax.optimization_barrier(near), arrived):
        got_square = squares(got, half)
        both = near_square + got_square
        here, there = lax.rsqrt(both), jnp.sqrt(got_square / both)
        got = own * here[:, :, None] + got[:, :half].astype(f32) * there[:, :, None]
        sums.append(got.astype(f16))
        sum_squares.append(both)
    packed = sums + [levels(jnp.concatenate(sum_squares, axis=1), width)]
    packed = jnp.concatenate(packed, axis=1)
    got = lax.all_to_all(packed, "dp", 0, 0, axis_index_groups=SAME_PARITY)
    square = squares(got, rows)
    back = jnp.sqrt(square / (jnp.sum(square, axis=0) / Z))
    logits = jnp.sum(got[:, :rows].astype(f32) * back[:, :, None], axis=0)

    logits = logits.reshape(2, half, width)
    here = 2 * lax.axis_index("tensor") + 2 * jnp.array([0, 1]) * (1 - 2 * core)
    here = (here * 2 + lax.axis_index("vocab")) * width
    target = jnp.stack([draft_map, map_other]) + jnp.arange(width, dtype=jnp.int32) + here[:, None]
    wanted = lax.dynamic_slice_in_dim(drafted, core * half, half)
    hit = wanted[None, :, None] == target[:, None, :]
    own_pick = jnp.sum(jnp.where(hit, logits, f32(0.0)), axis=(0, 2))
    own_top = jnp.max(logits, axis=(0, 2))
    own_total = jnp.sum(jnp.exp(logits - own_top[None, :, None]), axis=(0, 2))
    own = jnp.pad(jnp.stack([own_top, own_total, own_pick]), ((0, 5), (0, 128 - half)))
    logits = by_core(core, logits[0], swap_cores(logits[1]))
    every = lax.all_to_all(jnp.broadcast_to(own, (2 * PEERS,) + own.shape), PLANE, 0, 0)
    every = every[:, :3, :half].reshape(4, 2, 4, 3, half)
    top = jnp.max(every[:, :, :, 0], axis=(0, 2))
    total = every[:, :, :, 1] * jnp.exp(every[:, :, :, 0] - top[None, :, None])
    lse = (top + jnp.log(jnp.sum(total, axis=(0, 2)))).reshape(rows)
    picked = jnp.sum(every[:, :, :, 2], axis=(0, 2)).reshape(rows)
    return (logits - lse[:, None], picked - lse)


def solution(mesh):
    placed = (
        P("dp", ("tensor", "vocab")),
        P(("tensor", "vocab"), "dp"),
        P("dp"),
        P("dp", ("tensor", "vocab")),
        P(("tensor", "vocab")),
        P("dp"),
    )
    return jax.shard_map(
        body,
        mesh=mesh,
        in_specs=placed,
        out_specs=(P("dp", ("tensor", "vocab")), P("dp")),
        check_vma=False,
    )
```

```python
import jax
import jax.numpy as jnp
from jax import lax
from jax.sharding import PartitionSpec as P

eps = 1e-05
PLANE = ("tensor", "vocab")
f16, bf16, f32 = jnp.float16, jnp.bfloat16, jnp.float32

UP = 2.0**9
PARTIAL = 2.0**-2
LEVEL = 2.0**-7
FINE = 2.0**11

Z = 16
PEERS = 16
CORE_PAIRS = [(i, i ^ 1) for i in range(8)]
SAME_CORE = [[(2 * x + c) * 4 + y for x in range(4) for y in range(4)] for c in range(2)]
SAME_PARITY = [[2 * i + p for i in range(Z // 2)] for p in range(2)]


def swap_cores(a):
    return lax.ppermute(a, "tensor", CORE_PAIRS)


def by_core(core, mine, other):
    return jnp.where(
        core == 0, jnp.concatenate([mine, other]), jnp.concatenate([other, mine])
    )


def exchange(a):
    return lax.all_to_all(a, PLANE, 0, 0, axis_index_groups=SAME_CORE)


def pick(a, i):
    return lax.dynamic_index_in_dim(a, i, 1, keepdims=False)


def levels(square, width):
    root = jnp.sqrt(square) * LEVEL
    high = root.astype(f16)
    low = ((root - high.astype(f32)) * FINE).astype(f16)
    pair = jnp.stack([high, low], axis=-2)
    pad = [(0, 0)] * (pair.ndim - 2) + [(0, 6), (0, width - pair.shape[-1])]
    return jnp.pad(pair, pad)


def squares(a, rows):
    high, low = a[..., -8, :rows].astype(f32), a[..., -7, :rows].astype(f32)
    return ((high + low * (1.0 / FINE)) * (1.0 / LEVEL)) ** 2


def body(features, fc_weight, norm_gain, head_weight, draft_map, drafted):
    core = lax.axis_index("tensor") % 2
    parity = lax.axis_index("dp") % 2
    depth = fc_weight.shape[1]
    width = head_weight.shape[1]
    rows = features.shape[0]
    half = rows // 2

    sent = (features.astype(f32) * UP).astype(f16).reshape(2, half, -1)
    every = lax.all_gather(sent, "dp", axis=1)

    def joined_part(h):
        block = lax.dynamic_index_in_dim(every, h, 0, keepdims=False).astype(bf16)
        return jnp.dot(block, fc_weight, preferred_element_type=f32) * (PARTIAL / UP)

    away = joined_part(1 - core).astype(f16)
    kept = lax.optimization_barrier((joined_part(core), away))[0]
    chip = (kept + swap_cores(away).astype(f32)).astype(f16)
    later = lax.optimization_barrier((head_weight, draft_map, chip))
    head_other, map_other = swap_cores(later[0]), swap_cores(later[1])
    joined = jnp.sum(exchange(chip).astype(f32), axis=0)
    scaled = (joined * (norm_gain * (1.0 / PARTIAL))).astype(bf16)
    scaled = exchange(jnp.broadcast_to(scaled, (PEERS,) + scaled.shape))

    head = jnp.concatenate([head_weight, head_other], axis=1)
    gain, _, head = lax.optimization_barrier((norm_gain, map_other, head))
    own = scaled.astype(f32) * (1.0 / gain)
    square = (jnp.mean(own * own, axis=2) + eps).reshape(Z // 2, 2, half)
    scaled = scaled.reshape(Z // 2, 2, half, depth)

    def partial(h):
        block = pick(scaled, h).reshape(-1, depth)
        return jnp.dot(block, head, preferred_element_type=f32).reshape(-1, half, 2 * width)

    far_square, near_square = pick(square, 1 - parity), pick(square, parity)
    far = (partial(1 - parity) * lax.rsqrt(far_square)[:, :, None]).astype(f16)
    far_level = levels(far_square, width)
    near = lax.optimization_barrier(partial(parity))
    sums, sum_squares = [], []
    for v, by in ((0, 1), (1, -1)):
        part = slice(v * width, (v + 1) * width)
        got = jnp.concatenate([far[:, :, part], far_level], axis=1)
        got = lax.ppermute(got, "dp", [(i, (i + by) % Z) for i in range(Z)])
        got_square = squares(got, half)
        both = near_square + got_square
        here, there = lax.rsqrt(both), jnp.sqrt(got_square / both)
        got = near[:, :, part] * here[:, :, None] + got[:, :half].astype(f32) * there[:, :, None]
        sums.append(got.astype(f16))
        sum_squares.append(both)
    packed = sums + [levels(jnp.concatenate(sum_squares, axis=1), width)]
    packed = jnp.concatenate(packed, axis=1)
    got = lax.all_to_all(packed, "dp", 0, 0, axis_index_groups=SAME_PARITY)
    square = squares(got, rows)
    back = jnp.sqrt(square / (jnp.sum(square, axis=0) / Z))
    logits = jnp.sum(got[:, :rows].astype(f32) * back[:, :, None], axis=0)

    logits = logits.reshape(2, half, width)
    here = 2 * lax.axis_index("tensor") + 2 * jnp.array([0, 1]) * (1 - 2 * core)
    here = (here * 2 + lax.axis_index("vocab")) * width
    target = jnp.stack([draft_map, map_other]) + jnp.arange(width, dtype=jnp.int32) + here[:, None]
    wanted = lax.dynamic_slice_in_dim(drafted, core * half, half)
    hit = wanted[None, :, None] == target[:, None, :]
    own_pick = jnp.sum(jnp.where(hit, logits, f32(0.0)), axis=(0, 2))
    own_top = jnp.max(logits, axis=(0, 2))
    own_total = jnp.sum(jnp.exp(logits - own_top[None, :, None]), axis=(0, 2))
    own = jnp.pad(jnp.stack([own_top, own_total, own_pick]), ((0, 5), (0, 128 - half)))
    logits = by_core(core, logits[0], swap_cores(logits[1]))
    every = lax.all_to_all(jnp.broadcast_to(own, (2 * PEERS,) + own.shape), PLANE, 0, 0)
    every = every[:, :3, :half].reshape(4, 2, 4, 3, half)
    top = jnp.max(every[:, :, :, 0], axis=(0, 2))
    total = every[:, :, :, 1] * jnp.exp(every[:, :, :, 0] - top[None, :, None])
    lse = (top + jnp.log(jnp.sum(total, axis=(0, 2)))).reshape(rows)
    picked = jnp.sum(every[:, :, :, 2], axis=(0, 2)).reshape(rows)
    return (logits - lse[:, None], picked - lse)


def solution(mesh):
    placed = (
        P("dp", ("tensor", "vocab")),
        P(("tensor", "vocab"), "dp"),
        P("dp"),
        P("dp", ("tensor", "vocab")),
        P(("tensor", "vocab")),
        P("dp"),
    )
    return jax.shard_map(
        body,
        mesh=mesh,
        in_specs=placed,
        out_specs=(P("dp", ("tensor", "vocab")), P("dp")),
        check_vma=False,
    )
```

```python
import jax
import jax.numpy as jnp
from jax import lax
from jax.sharding import PartitionSpec as P

eps = 1e-05
PLANE = ("tensor", "vocab")
f16, bf16, f32 = jnp.float16, jnp.bfloat16, jnp.float32

UP = 2.0**9
PARTIAL = 2.0**-2
LEVEL = 2.0**-7
FINE = 2.0**11

Z = 16
PEERS = 16
CORE_PAIRS = [(i, i ^ 1) for i in range(8)]
SAME_CORE = [[(2 * x + c) * 4 + y for x in range(4) for y in range(4)] for c in range(2)]
SAME_PARITY = [[2 * i + p for i in range(Z // 2)] for p in range(2)]


def swap_cores(a):
    return lax.ppermute(a, "tensor", CORE_PAIRS)


def by_core(core, mine, other):
    return jnp.where(
        core == 0, jnp.concatenate([mine, other]), jnp.concatenate([other, mine])
    )


def exchange(a):
    return lax.all_to_all(a, PLANE, 0, 0, axis_index_groups=SAME_CORE)


def pick(a, i):
    return lax.dynamic_index_in_dim(a, i, 1, keepdims=False)


def levels(square, width):
    root = jnp.sqrt(square) * LEVEL
    high = root.astype(f16)
    low = ((root - high.astype(f32)) * FINE).astype(f16)
    pair = jnp.stack([high, low], axis=-2)
    pad = [(0, 0)] * (pair.ndim - 2) + [(0, 6), (0, width - pair.shape[-1])]
    return jnp.pad(pair, pad)


def squares(a, rows):
    high, low = a[..., -8, :rows].astype(f32), a[..., -7, :rows].astype(f32)
    return ((high + low * (1.0 / FINE)) * (1.0 / LEVEL)) ** 2


def body(features, fc_weight, norm_gain, head_weight, draft_map, drafted):
    core = lax.axis_index("tensor") % 2
    parity = lax.axis_index("dp") % 2
    depth = fc_weight.shape[1]
    width = head_weight.shape[1]
    rows = features.shape[0]
    half = rows // 2

    sent = (features.astype(f32) * UP).astype(f16).reshape(2, half, -1)
    every = lax.all_gather(sent, "dp", axis=1)

    def joined_part(h):
        block = lax.dynamic_index_in_dim(every, h, 0, keepdims=False).astype(bf16)
        return jnp.dot(block, fc_weight, preferred_element_type=f32) * (PARTIAL / UP)

    away = joined_part(1 - core).astype(f16)
    kept = lax.optimization_barrier((joined_part(core), away))[0]
    chip = (kept + swap_cores(away).astype(f32)).astype(f16)
    later = lax.optimization_barrier((head_weight, draft_map, chip))
    head_other, map_other = swap_cores(later[0]), swap_cores(later[1])
    joined = jnp.sum(exchange(chip).astype(f32), axis=0)
    scaled = (joined * (norm_gain * (1.0 / PARTIAL))).astype(bf16)
    scaled = exchange(jnp.broadcast_to(scaled, (PEERS,) + scaled.shape))

    head = jnp.concatenate([head_weight, head_other], axis=1)
    gain, _, head = lax.optimization_barrier((norm_gain, map_other, head))
    scaled = scaled.reshape(Z // 2, 2, half, depth)

    def side(h):
        block = pick(scaled, h)
        own = block.astype(f32) * (1.0 / gain)
        values = jnp.dot(block.reshape(-1, depth), head, preferred_element_type=f32)
        return jnp.mean(own * own, axis=2) + eps, values.reshape(-1, half, 2 * width)

    far_square, far = side(1 - parity)
    far = (far * lax.rsqrt(far_square)[:, :, None]).astype(f16)
    far_level = levels(far_square, width)
    near_square, near = lax.optimization_barrier(side(lax.optimization_barrier((parity, far))[0]))
    sums, sum_squares = [], []
    for v, by in ((0, 1), (1, -1)):
        part = slice(v * width, (v + 1) * width)
        got = jnp.concatenate([far[:, :, part], far_level], axis=1)
        got = lax.ppermute(got, "dp", [(i, (i + by) % Z) for i in range(Z)])
        got_square = squares(got, half)
        both = near_square + got_square
        here, there = lax.rsqrt(both), jnp.sqrt(got_square / both)
        got = near[:, :, part] * here[:, :, None] + got[:, :half].astype(f32) * there[:, :, None]
        sums.append(got.astype(f16))
        sum_squares.append(both)
    packed = sums + [levels(jnp.concatenate(sum_squares, axis=1), width)]
    packed = jnp.concatenate(packed, axis=1)
    got = lax.all_to_all(packed, "dp", 0, 0, axis_index_groups=SAME_PARITY)
    square = squares(got, rows)
    back = jnp.sqrt(square / (jnp.sum(square, axis=0) / Z))
    logits = jnp.sum(got[:, :rows].astype(f32) * back[:, :, None], axis=0)

    logits = logits.reshape(2, half, width)
    here = 2 * lax.axis_index("tensor") + 2 * jnp.array([0, 1]) * (1 - 2 * core)
    here = (here * 2 + lax.axis_index("vocab")) * width
    target = jnp.stack([draft_map, map_other]) + jnp.arange(width, dtype=jnp.int32) + here[:, None]
    wanted = lax.dynamic_slice_in_dim(drafted, core * half, half)
    hit = wanted[None, :, None] == target[:, None, :]
    own_pick = jnp.sum(jnp.where(hit, logits, f32(0.0)), axis=(0, 2))
    own_top = jnp.max(logits, axis=(0, 2))
    own_total = jnp.sum(jnp.exp(logits - own_top[None, :, None]), axis=(0, 2))
    own = jnp.pad(jnp.stack([own_top, own_total, own_pick]), ((0, 5), (0, 128 - half)))
    logits = by_core(core, logits[0], swap_cores(logits[1]))
    every = lax.all_to_all(jnp.broadcast_to(own, (2 * PEERS,) + own.shape), PLANE, 0, 0)
    every = every[:, :3, :half].reshape(4, 2, 4, 3, half)
    top = jnp.max(every[:, :, :, 0], axis=(0, 2))
    total = every[:, :, :, 1] * jnp.exp(every[:, :, :, 0] - top[None, :, None])
    lse = (top + jnp.log(jnp.sum(total, axis=(0, 2)))).reshape(rows)
    picked = jnp.sum(every[:, :, :, 2], axis=(0, 2)).reshape(rows)
    return (logits - lse[:, None], picked - lse)


def solution(mesh):
    placed = (
        P("dp", ("tensor", "vocab")),
        P(("tensor", "vocab"), "dp"),
        P("dp"),
        P("dp", ("tensor", "vocab")),
        P(("tensor", "vocab")),
        P("dp"),
    )
    return jax.shard_map(
        body,
        mesh=mesh,
        in_specs=placed,
        out_specs=(P("dp", ("tensor", "vocab")), P("dp")),
        check_vma=False,
    )
```
